256 devices in a mesh: vol: 16 (over z, y_lo), ctl: 16 (over x, y_hi, core).
Axes of the slice: x: 4, y: 4 (y_hi: 2, y_lo: 2; y = y_hi * 2 + y_lo), z: 8, core: 2. Of those that a mesh axis runs over, the one named last changes fastest.
Arguments:
- node_points: float32 [3, 16, 32768], P(None, 'vol', 'ctl'), may hold values from -0.6 to 0.6
- cotangent: float32 [3, 16, 32768], P(None, 'vol', 'ctl'), may hold values from -6 to 6
- ctl_points: float32 [3, 16, 256], P(None, 'ctl', 'vol'), may hold values from -0.6 to 0.6
- ctl_weights: float32 [3, 16, 256], P(None, 'ctl', 'vol'), may hold values from -6 to 6
- tile_mask: int32 [16, 256, 16, 2], P('vol', None, 'ctl'), may hold values 0 or 1
Outputs:
- node_grad: float32 [3, 16, 32768], P(None, 'vol', 'ctl')
- weight_grad: float32 [3, 16, 256], P(None, 'ctl', 'vol')
- control_grad: float32 [3, 16, 256], P(None, 'ctl', 'vol')
The draws below stay inside these ranges and needn't reach their ends.
All inputs are finite; a program needn't handle non-finite values. No bound on the sum of `tile_mask` on one device may be relied on, other than what follows from the above.
Results may differ from the reference program's by a relative error of at most 0.0001.
Values sent between devices are 32-bit elements; how exact they have to be, the bound alone decides.
No kernel may reach another device: no remote copies, remote signals or barrier semaphores. Data moves between devices by JAX's collectives and lax.ppermute only.
A program may use at most 192 MiB of HBM per device.

```python
import math
import jax
import jax.numpy as jnp
from jax import lax

VD = 32768
CD = 256
TILE = 128
NV = 524288
NC = 4096
N_VOL = 16
N_CTL = 16


def set_ends(array, key, least, largest):
    place = [jax.random.randint(jax.random.fold_in(key, axis), (), 0, length) for axis, length in enumerate(array.shape)]
    longest = array.shape.index(max(array.shape))
    beside = place[:longest] + [(place[longest] + 1) % array.shape[longest]] + place[longest + 1:]
    return array.at[tuple(place)].set(least).at[tuple(beside)].set(largest)


def block_scale(stream_key, extent, cuts, low, top_value):
    factor_of = 1.0
    for position, blocks in cuts:
        steps = jax.random.uniform(jax.random.fold_in(jax.random.fold_in(stream_key, 6), position), (blocks,), jnp.float32, low / len(cuts), top_value / len(cuts))
        factor_of = factor_of * jnp.repeat(jnp.exp(steps), extent[position] // blocks).reshape((-1,) + (1,) * (len(extent) - 1 - position))
    return factor_of


def normal_values(key, shape, spread, limit, split=(), held_as=jnp.bfloat16):
    array = jax.random.normal(key, shape, jnp.float32) * spread
    if len(split) > 0:
        array = block_scale(key, shape, split, -0.22, 0.18) * array
    return jnp.clip(array, min=-limit, max=limit).astype(held_as)


def setup_inputs(seed: int = 0) -> dict:
    seeds = jax.random.split(jax.random.key(seed), 6)
    return {
        "node_points": jnp.clip(jax.random.uniform(seeds[0], (3, N_VOL, VD), jnp.float32, -0.6, 0.6) * block_scale(seeds[0], (3, N_VOL, VD), ((1, 16), (2, 16)), -0.4, 0.0), -0.6, 0.6),
        "cotangent": normal_values(seeds[1], (3, N_VOL, VD), 1.0, 6.0, ((1, 16), (2, 16)), jnp.float32),
        "ctl_points": jnp.clip(jax.random.uniform(seeds[2], (3, N_CTL, CD), jnp.float32, -0.6, 0.6) * block_scale(seeds[2], (3, N_CTL, CD), ((1, 16), (2, 16)), -0.4, 0.0), -0.6, 0.6),
        "ctl_weights": normal_values(seeds[3], (3, N_CTL, CD), 1.0, 6.0, ((1, 16), (2, 16)), jnp.float32),
        "tile_mask": set_ends((jax.random.randint(seeds[4], (N_VOL, VD // TILE, N_CTL, CD // TILE), 0, 4) < 3).astype(jnp.int32), jax.random.fold_in(seeds[4], 1), 0, 1),
    }


def tile_gradients(nodes, cots, ctl, wts, tiles, tile, pairs):
    rows = nodes.shape[1]
    cols = ctl.shape[1]
    units = rows // tile
    wanted = max(1, pairs // (cols * tile))
    factor = max([d for d in range(1, min(units, wanted) + 1) if units % d == 0])
    block = factor * tile
    count = rows // block
    tcols = tiles.shape[1]
    node_blocks = nodes.reshape(3, count, block).transpose(1, 0, 2)
    cot_blocks = cots.reshape(3, count, block).transpose(1, 0, 2)
    tile_blocks = tiles.reshape(count, factor, tcols)

    def step(carry, items):
        acc_w, acc_y = carry
        xb, gb, tb = items
        diff = xb[:, :, None] - ctl[:, None, :]
        dist = jnp.sqrt(lax.optimization_barrier(jnp.sum(diff * diff, axis=0)))
        near = jnp.maximum(1.0 - dist, 0.0)
        maskf = jnp.broadcast_to(tb.astype(jnp.float32)[:, None, :, None], (factor, tile, tcols, tile)).reshape(block, cols)
        near3 = near * near * near
        phi = maskf * near3 * near * (4.0 * dist + 1.0)
        align = gb[0][:, None] * wts[0][None, :] + gb[1][:, None] * wts[1][None, :] + gb[2][:, None] * wts[2][None, :]
        force = maskf * -20.0 * near3 * align
        pulled = force[None] * diff
        node_part = lax.optimization_barrier(jnp.sum(pulled, axis=2))
        acc_w = acc_w + lax.optimization_barrier(jnp.sum(phi[None] * gb[:, :, None], axis=1))
        acc_y = acc_y - lax.optimization_barrier(jnp.sum(pulled, axis=1))
        return ((acc_w, acc_y), node_part)
    zeros = jnp.zeros((3, cols), jnp.float32)
    (acc_w, acc_y), parts = lax.scan(step, (zeros, zeros), (node_blocks, cot_blocks, tile_blocks))
    node_part = parts.transpose(1, 0, 2).reshape(3, rows)
    return (node_part, acc_w, acc_y)

def reference(node_points, cotangent, ctl_points, ctl_weights, tile_mask):
    nodes = node_points.reshape(3, NV)
    cots = cotangent.reshape(3, NV)
    ctl = ctl_points.reshape(3, NC)
    wts = ctl_weights.reshape(3, NC)
    tiles = tile_mask.reshape(NV // TILE, NC // TILE)
    node_part, acc_w, acc_y = tile_gradients(nodes, cots, ctl, wts, tiles, TILE, 4194304)
    node_grad = (node_part * (1.0 / math.sqrt(NC))).reshape(3, N_VOL, VD)
    weight_grad = (acc_w * (1.0 / math.sqrt(NV))).reshape(3, N_CTL, CD)
    control_grad = (acc_y * (1.0 / math.sqrt(NV))).reshape(3, N_CTL, CD)
    return (node_grad, weight_grad, control_grad)
```

```python
import functools
import math

import jax
import jax.numpy as jnp
from jax import lax
from jax.experimental import pallas as pl
from jax.experimental.pallas import tpu as pltpu
from jax.sharding import PartitionSpec as P

TILE = 128
GROUP = 4
NODE_BITS = (8, 2, 4, 1)
CTL_BITS = (1, 2, 4, 8)
f32 = jnp.float32


def offset(place):
    return sum(bit for k, bit in enumerate(NODE_BITS) if place >> k & 1)


def swap(value, axis, bit):
    return lax.ppermute(value, axis, [(i, i ^ bit) for i in range(lax.axis_size(axis))])


def list_kernel(where_ref, mask_ref, list_ref, count_ref, *, places, units):
    tiles = places * units
    mine = where_ref[0]
    for half in range(2):
        n = jnp.int32(0)
        column = half ^ where_ref[1]
        for place in range(places):
            row = (mine ^ offset(place)) * units

            def step(k, n, place=place, row=row, column=column, half=half):
                list_ref[half, n] = place * units + k
                return n + jnp.where(mask_ref[row + k, column] != 0, 1, 0)

            n = lax.fori_loop(0, units, step, n, unroll=True)
        for k in range(GROUP):
            list_ref[half, n + k] = tiles
        count_ref[half] = (n + GROUP - 1) // GROUP


def pair_kernel(count_ref, list_ref, nod_ref, ctl_ref, send_ref, keep_ref, csum_ref, node_ref, acc_ref, *, tiles):
    node_ref[...] = jnp.zeros_like(node_ref)
    acc_ref[...] = jnp.zeros_like(acc_ref)
    for half in range(2):

        def body(i, _, half=half):
            ts = [list_ref[half, i * GROUP + b] for b in range(GROUP)]
            xg = [[jnp.broadcast_to(nod_ref[k, pl.ds(t, 1), :], (8, TILE)) for k in range(6)] for t in ts]
            node_sum = [[None] * 3 for _ in range(GROUP)]
            for c in range(TILE // 8):
                rows = pl.ds(half * TILE + c * 8, 8)
                yw = [ctl_ref[k, rows, :] for k in range(6)]
                ctl_sum = [None] * 6
                for b in range(GROUP):
                    x = xg[b][:3]
                    g = xg[b][3:]
                    diff = [x[k] - yw[k] for k in range(3)]
                    square = diff[0] * diff[0] + diff[1] * diff[1] + diff[2] * diff[2]
                    square = jnp.maximum(square, 1e-30)
                    dist = square * lax.rsqrt(square)
                    near = jnp.maximum(1.0 - dist, 0.0)
                    near2 = near * near
                    phi = near2 * near2 * (dist + 0.25)
                    align = g[0] * yw[3] + g[1] * yw[4] + g[2] * yw[5]
                    force = near2 * near * align
                    for k in range(3):
                        pulled = force * diff[k]
                        pushed = phi * g[k]
                        node_sum[b][k] = pulled if c == 0 else node_sum[b][k] + pulled
                        ctl_sum[3 + k] = pulled if b == 0 else ctl_sum[3 + k] + pulled
                        ctl_sum[k] = pushed if b == 0 else ctl_sum[k] + pushed
                for k in range(6):
                    acc_ref[k, rows, :] += ctl_sum[k]
            for b in range(GROUP):
                for k in range(3):
                    node_ref[k, pl.ds(ts[b], 1), :] += jnp.sum(node_sum[b][k], axis=0, keepdims=True)
            return 0

        lax.fori_loop(0, count_ref[half], body, 0)
    keep_ref[...] = node_ref[:, : tiles // 2, :]
    send_ref[...] = node_ref[:, tiles // 2 : tiles, :]
    ones = jnp.ones((8, TILE), f32)
    for k in range(6):
        total = lax.dot_general(
            ones, acc_ref[k], (((1,), (1,)), ((), ())), precision=lax.Precision.HIGHEST, preferred_element_type=f32
        )
        csum_ref[pl.ds(k, 1), :] = total[:1]


def local(node_points, cotangent, ctl_points, ctl_weights, tile_mask):
    n_vol = lax.axis_size("vol")
    n_ctl = lax.axis_size("ctl")
    own = node_points.shape[2]
    units = own // TILE
    tiles = units * n_ctl
    part = ctl_points.shape[2]
    width = part * n_vol
    total_nodes = own * n_ctl * n_vol
    total_ctl = width * n_ctl
    where = jnp.stack([lax.axis_index("ctl"), lax.axis_index("vol") * part // TILE]).astype(jnp.int32)

    nod = jnp.concatenate([node_points, cotangent], axis=0).reshape(6, units, TILE)
    ctl = jnp.concatenate([ctl_points, ctl_weights], axis=0).reshape(6, part)
    for node_bit, ctl_bit in zip(NODE_BITS, CTL_BITS):
        nod_new = swap(nod, "ctl", node_bit)
        ctl_new = swap(ctl, "vol", ctl_bit)
        nod = jnp.concatenate([nod, nod_new], axis=1)
        ctl = jnp.concatenate([ctl, ctl_new], axis=1)

    vmem = pl.BlockSpec(memory_space=pltpu.VMEM)
    smem = pl.BlockSpec(memory_space=pltpu.SMEM)
    lists, counts = pl.pallas_call(
        functools.partial(list_kernel, places=n_ctl, units=units),
        out_shape=(jax.ShapeDtypeStruct((2, tiles + 8), jnp.int32), jax.ShapeDtypeStruct((2,), jnp.int32)),
        in_specs=[smem, smem],
        out_specs=(smem, smem),
        name="kept_tiles",
    )(where, tile_mask.reshape(tiles, 2))
    send, keep, csum = pl.pallas_call(
        functools.partial(pair_kernel, tiles=tiles),
        out_shape=(
            jax.ShapeDtypeStruct((3, tiles // 2, TILE), f32),
            jax.ShapeDtypeStruct((3, tiles // 2, TILE), f32),
            jax.ShapeDtypeStruct((6, width), f32),
        ),
        in_specs=[smem, smem, vmem, vmem],
        out_specs=(vmem, vmem, vmem),
        scratch_shapes=[pltpu.VMEM((3, tiles + 8, TILE), f32), pltpu.VMEM((6, width, TILE), f32)],
        compiler_params=pltpu.CompilerParams(vmem_limit_bytes=32 << 20),
        name="pairs",
    )(
        counts,
        lists,
        jnp.pad(nod, ((0, 0), (0, 8), (0, 0))),
        jnp.broadcast_to(ctl[:, :, None], (6, width, TILE)),
    )
    size, span = tiles // 2, width // 2
    csend, ckeep = csum[:, span:], csum[:, :span]
    for node_bit, ctl_bit in zip(NODE_BITS[::-1], CTL_BITS[::-1]):
        send = swap(send, "ctl", node_bit)
        csend = swap(csend, "vol", ctl_bit)
        size, span = size // 2, span // 2
        if size >= units:
            send, keep = keep[:, size:] + send[:, size:], keep[:, :size] + send[:, :size]
            csend, ckeep = ckeep[:, span:] + csend[:, span:], ckeep[:, :span] + csend[:, :span]
        else:
            keep, ckeep = keep + send, ckeep + csend
    node_grad = keep.reshape(3, 1, own) * (-20.0 / math.sqrt(total_ctl))
    weight_grad = ckeep[:3].reshape(3, 1, part) * (4.0 / math.sqrt(total_nodes))
    control_grad = ckeep[3:].reshape(3, 1, part) * (20.0 / math.sqrt(total_nodes))
    return (node_grad, weight_grad, control_grad)


def solution(mesh):
    nodes = P(None, "vol", "ctl")
    ctl = P(None, "ctl", "vol")
    return jax.shard_map(
        local,
        mesh=mesh,
        in_specs=(nodes, nodes, ctl, ctl, P("vol", None, "ctl", None)),
        out_specs=(nodes, ctl, ctl),
        check_vma=False,
    )
```

```python
import functools
import math

import jax
import jax.numpy as jnp
from jax import lax
from jax.experimental import pallas as pl
from jax.experimental.pallas import tpu as pltpu
from jax.sharding import PartitionSpec as P

TILE = 128
GROUP = 4
SHIFT = 1024
NODE_BITS = (12, 2, 4, 1)
CTL_BITS = (12, 4, 2, 1)
SUM_BITS = (12, 2, 4, 1)
CALLS = ((8, 8), (0, 8))
f32 = jnp.float32


def xor_of(bits, index):
    return functools.reduce(lambda a, b: a ^ b, [bit for k, bit in enumerate(bits) if index >> k & 1], 0)


def offset(slot):
    return xor_of(SUM_BITS[::-1], slot)


def place(slot):
    return [xor_of(NODE_BITS, p) for p in range(1 << len(NODE_BITS))].index(offset(slot))


def swap(value, axis, bit):
    return lax.ppermute(value, axis, [(i, i ^ bit) for i in range(lax.axis_size(axis))])


def list_kernel(where_ref, mask_ref, list_ref, count_ref, *, units, stride):
    lists = [(call, half) for call in range(len(CALLS)) for half in range(2)]
    found = [jnp.int32(j * stride) for j in range(len(lists))]
    columns = [half ^ where_ref[1] for half in range(2)]
    for i in range(max(blocks for _, blocks in CALLS)):
        live = [j for j, (call, _) in enumerate(lists) if i < CALLS[call][1]]
        rows = {}
        for j in live:
            call, half = lists[j]
            rows[j] = (where_ref[0] ^ offset(CALLS[call][0] + i)) * (2 * units) + columns[half]
        for k in range(units):
            for j in live:
                call, half = lists[j]
                list_ref[found[j]] = (place(CALLS[call][0] + i) * units + k) * SHIFT + i * units + k
                found[j] = found[j] + mask_ref[rows[j] + 2 * k]
    for j, (call, half) in enumerate(lists):
        for k in range(GROUP):
            list_ref[found[j] + k] = (units << len(NODE_BITS)) * SHIFT + CALLS[call][1] * units
        count_ref[j] = (found[j] - j * stride + GROUP - 1) // GROUP


def pair_kernel(count_ref, list_ref, nod_ref, ctl_ref, before_ref, part_ref, csum_ref, node_ref, acc_ref, *, call, stride, part):
    node_ref[...] = jnp.zeros_like(node_ref)
    acc_ref[...] = jnp.zeros_like(acc_ref)
    for half in range(2):
        row = 2 * call + half
        starts = [s for s in range(0, acc_ref.shape[1], 8) if s // part % 2 == half]

        def body(i, _, row=row, starts=starts):
            items = [list_ref[row * stride + i * GROUP + b] for b in range(GROUP)]
            ts = [item >> 10 for item in items]
            outs = [item & (SHIFT - 1) for item in items]
            xg = [[jnp.broadcast_to(nod_ref[k, pl.ds(t, 1), :], (8, TILE)) for k in range(6)] for t in ts]
            node_sum = [[None] * 3 for _ in range(GROUP)]
            for c, start in enumerate(starts):
                rows = pl.ds(start, 8)
                yw = [ctl_ref[k, rows, :] for k in range(6)]
                ctl_sum = [None] * 6
                for b in range(GROUP):
                    x = xg[b][:3]
                    g = xg[b][3:]
                    diff = [x[k] - yw[k] for k in range(3)]
                    square = diff[0] * diff[0] + diff[1] * diff[1] + diff[2] * diff[2]
                    dist = pl.reciprocal(lax.rsqrt(square), approx=True)
                    near = jnp.maximum(1.0 - dist, 0.0)
                    near2 = near * near
                    phi = near2 * near2 * (dist + 0.25)
                    align = g[0] * yw[3] + g[1] * yw[4] + g[2] * yw[5]
                    force = near2 * near * align
                    for k in range(3):
                        pulled = force * diff[k]
                        pushed = phi * g[k]
                        node_sum[b][k] = pulled if c == 0 else node_sum[b][k] + pulled
                        ctl_sum[3 + k] = pulled if b == 0 else ctl_sum[3 + k] + pulled
                        ctl_sum[k] = pushed if b == 0 else ctl_sum[k] + pushed
                for k in range(6):
                    acc_ref[k, rows, :] += ctl_sum[k]
            for b in range(GROUP):
                for k in range(3):
                    node_ref[k, pl.ds(outs[b], 1), :] += jnp.sum(node_sum[b][k], axis=0, keepdims=True)
            return 0

        lax.fori_loop(0, count_ref[row], body, 0)
    part_ref[...] = node_ref[:, : part_ref.shape[1], :]
    for k in range(6):
        for s in range(0, acc_ref.shape[1], TILE):
            total = jnp.sum(acc_ref[k, pl.ds(s, TILE), :].T, axis=0, keepdims=True)
            csum_ref[pl.ds(k, 1), pl.ds(s, TILE)] = before_ref[pl.ds(k, 1), pl.ds(s, TILE)] + total


def local(node_points, cotangent, ctl_points, ctl_weights, tile_mask):
    n_vol = lax.axis_size("vol")
    n_ctl = lax.axis_size("ctl")
    own = node_points.shape[2]
    units = own // TILE
    tiles = units * n_ctl
    part = ctl_points.shape[2]
    width = part * n_vol
    total_nodes = own * n_ctl * n_vol
    total_ctl = width * n_ctl
    vmem = pl.BlockSpec(memory_space=pltpu.VMEM)
    smem = pl.BlockSpec(memory_space=pltpu.SMEM)
    stride = max(blocks for _, blocks in CALLS) * units + 8
    where = jnp.stack([lax.axis_index("ctl"), lax.axis_index("vol") * part // TILE]).astype(jnp.int32)
    mask = tile_mask.reshape(2 * tiles)

    nod = jnp.concatenate([node_points, cotangent], axis=0).reshape(6, units, TILE)
    ctl = jnp.concatenate([ctl_points, ctl_weights], axis=0).reshape(6, part)
    for step, (node_bit, ctl_bit) in enumerate(zip(NODE_BITS, CTL_BITS)):
        nod_new = swap(nod, "ctl", node_bit)
        ctl_new = swap(ctl, "vol", ctl_bit)
        if step == 1:
            nod_new, where, mask = lax.optimization_barrier((nod_new, where, mask))
        if step == 2:
            lists, counts = pl.pallas_call(
                functools.partial(list_kernel, units=units, stride=stride),
                out_shape=(
                    jax.ShapeDtypeStruct((2 * len(CALLS) * stride,), jnp.int32),
                    jax.ShapeDtypeStruct((2 * len(CALLS),), jnp.int32),
                ),
                in_specs=[smem, smem],
                out_specs=(smem, smem),
                name="kept_tiles",
            )(where, mask)
            nod_new, lists, counts = lax.optimization_barrier((nod_new, lists, counts))
        nod = jnp.concatenate([nod, nod_new], axis=1)
        ctl = jnp.concatenate([ctl, ctl_new], axis=1)
    nod = jnp.pad(nod, ((0, 0), (0, 8), (0, 0)))
    ctl = jnp.broadcast_to(ctl[:, :, None], (6, width, TILE))

    def pairs(call, csum):
        rows = CALLS[call][1] * units
        work = rows * TILE * width
        return pl.pallas_call(
            functools.partial(pair_kernel, call=call, stride=stride, part=part),
            out_shape=(jax.ShapeDtypeStruct((3, rows, TILE), f32), jax.ShapeDtypeStruct((6, width), f32)),
            in_specs=[smem, smem, vmem, vmem, vmem],
            out_specs=(vmem, vmem),
            scratch_shapes=[pltpu.VMEM((3, rows + 8, TILE), f32), pltpu.VMEM((6, width, TILE), f32)],
            compiler_params=pltpu.CompilerParams(vmem_limit_bytes=32 << 20),
            cost_estimate=pl.CostEstimate(flops=5000 * work, bytes_accessed=16 * work, transcendentals=work),
            name="pairs",
        )(counts, lists, nod, ctl, csum)

    mine, csum = pairs(0, jnp.zeros((6, width), f32))
    got = []
    for step in range(1, len(CALLS)):
        got = [g[:, g.shape[1] // 2 :] for g in got], [g[:, : g.shape[1] // 2] for g in got]
        sent = swap(sum(got[0], mine), "ctl", SUM_BITS[step - 1])
        mine, csum = pairs(step, csum)
        csum, sent = lax.optimization_barrier((csum, sent))
        got = got[1] + [sent]
    keep = sum(got, mine)
    ckeep = csum
    node_bits = SUM_BITS[len(CALLS) - 1 :]
    for step, bit in enumerate(CTL_BITS[::-1]):
        span = ckeep.shape[1] // 2
        csend = swap(ckeep[:, span:], "vol", bit)
        if step < len(node_bits):
            size = keep.shape[1] // 2
            send = swap(keep[:, size:], "ctl", node_bits[step])
            csend, send = lax.optimization_barrier((csend, send))
            keep = keep[:, :size] + send
        ckeep = ckeep[:, :span] + csend
    node_grad = keep.reshape(3, 1, own) * (-20.0 / math.sqrt(total_ctl))
    weight_grad = ckeep[:3].reshape(3, 1, part) * (4.0 / math.sqrt(total_nodes))
    control_grad = ckeep[3:].reshape(3, 1, part) * (20.0 / math.sqrt(total_nodes))
    return (node_grad, weight_grad, control_grad)


def solution(mesh):
    nodes = P(None, "vol", "ctl")
    ctl = P(None, "ctl", "vol")
    return jax.shard_map(
        local,
        mesh=mesh,
        in_specs=(nodes, nodes, ctl, ctl, P("vol", None, "ctl", None)),
        out_specs=(nodes, ctl, ctl),
        check_vma=False,
    )
```

```python
import functools
import math

import jax
import jax.numpy as jnp
from jax import lax
from jax.experimental import pallas as pl
from jax.experimental.pallas import tpu as pltpu
from jax.sharding import PartitionSpec as P

TILE = 128
GROUP = 4
SHIFT = 1024
NODE_BITS = (12, 2, 4, 1)
CTL_BITS = (12, 4, 2, 1)
SUM_BITS = (12, 2, 4, 1)
CALLS = ((8, 8), (0, 8))
f32 = jnp.float32


def xor_of(bits, index):
    return functools.reduce(lambda a, b: a ^ b, [bit for k, bit in enumerate(bits) if index >> k & 1], 0)


def offset(slot):
    return xor_of(SUM_BITS[::-1], slot)


def place(slot):
    return [xor_of(NODE_BITS, p) for p in range(1 << len(NODE_BITS))].index(offset(slot))


def swap(value, axis, bit):
    return lax.ppermute(value, axis, [(i, i ^ bit) for i in range(lax.axis_size(axis))])


def list_kernel(where_ref, mask_ref, list_ref, count_ref, *, units, stride):
    lists = [(call, half) for call in range(len(CALLS)) for half in range(2)]
    found = [jnp.int32(j * stride) for j in range(len(lists))]
    columns = [half ^ where_ref[1] for half in range(2)]
    for i in range(max(blocks for _, blocks in CALLS)):
        live = [j for j, (call, _) in enumerate(lists) if i < CALLS[call][1]]
        rows = {}
        for j in live:
            call, half = lists[j]
            rows[j] = (where_ref[0] ^ offset(CALLS[call][0] + i)) * (2 * units) + columns[half]
        for k in range(units):
            for j in live:
                call, half = lists[j]
                list_ref[found[j]] = (place(CALLS[call][0] + i) * units + k) * SHIFT + i * units + k
                found[j] = found[j] + mask_ref[rows[j] + 2 * k]
    for j in range(len(lists)):
        count_ref[j] = found[j] - j * stride


def pair_kernel(count_ref, list_ref, nod_ref, ctl_ref, before_ref, part_ref, csum_ref, node_ref, acc_ref, *, call, stride, part):
    node_ref[...] = jnp.zeros_like(node_ref)
    acc_ref[...] = jnp.zeros_like(acc_ref)
    for half in range(2):
        row = 2 * call + half
        starts = [s for s in range(0, acc_ref.shape[1], 8) if s // part % 2 == half]

        def body(first, size, row=row, starts=starts):
            items = [list_ref[row * stride + first + b] for b in range(size)]
            ts = [item >> 10 for item in items]
            outs = [item & (SHIFT - 1) for item in items]
            xg = [[jnp.broadcast_to(nod_ref[k, pl.ds(t, 1), :], (8, TILE)) for k in range(6)] for t in ts]
            node_sum = [[None] * 3 for _ in range(size)]
            for c, start in enumerate(starts):
                rows = pl.ds(start, 8)
                yw = [ctl_ref[k, rows, :] for k in range(6)]
                ctl_sum = [None] * 6
                for b in range(size):
                    x = xg[b][:3]
                    g = xg[b][3:]
                    diff = [x[k] - yw[k] for k in range(3)]
                    square = diff[0] * diff[0] + diff[1] * diff[1] + diff[2] * diff[2]
                    dist = pl.reciprocal(lax.rsqrt(square), approx=True)
                    near = jnp.maximum(1.0 - dist, 0.0)
                    near2 = near * near
                    phi = near2 * near2 * (dist + 0.25)
                    align = g[0] * yw[3] + g[1] * yw[4] + g[2] * yw[5]
                    force = near2 * near * align
                    for k in range(3):
                        pulled = force * diff[k]
                        pushed = phi * g[k]
                        node_sum[b][k] = pulled if c == 0 else node_sum[b][k] + pulled
                        ctl_sum[3 + k] = pulled if b == 0 else ctl_sum[3 + k] + pulled
                        ctl_sum[k] = pushed if b == 0 else ctl_sum[k] + pushed
                for k in range(6):
                    acc_ref[k, rows, :] += ctl_sum[k]
            for b in range(size):
                for k in range(3):
                    node_ref[k, pl.ds(outs[b], 1), :] += jnp.sum(node_sum[b][k], axis=0, keepdims=True)

        def group(i, _, body=body):
            body(i * GROUP, GROUP)
            return 0

        def single(i, _, body=body):
            body(i, 1)
            return 0

        count = count_ref[row]
        lax.fori_loop(0, count // GROUP, group, 0)
        lax.fori_loop(count // GROUP * GROUP, count, single, 0)
    part_ref[...] = node_ref[:, : part_ref.shape[1], :]
    for k in range(6):
        for s in range(0, acc_ref.shape[1], TILE):
            total = jnp.sum(acc_ref[k, pl.ds(s, TILE), :].T, axis=0, keepdims=True)
            csum_ref[pl.ds(k, 1), pl.ds(s, TILE)] = before_ref[pl.ds(k, 1), pl.ds(s, TILE)] + total


def local(node_points, cotangent, ctl_points, ctl_weights, tile_mask):
    n_vol = lax.axis_size("vol")
    n_ctl = lax.axis_size("ctl")
    own = node_points.shape[2]
    units = own // TILE
    tiles = units * n_ctl
    part = ctl_points.shape[2]
    width = part * n_vol
    total_nodes = own * n_ctl * n_vol
    total_ctl = width * n_ctl
    vmem = pl.BlockSpec(memory_space=pltpu.VMEM)
    smem = pl.BlockSpec(memory_space=pltpu.SMEM)
    stride = max(blocks for _, blocks in CALLS) * units + 8
    where = jnp.stack([lax.axis_index("ctl"), lax.axis_index("vol") * part // TILE]).astype(jnp.int32)
    mask = tile_mask.reshape(2 * tiles)

    nod = jnp.concatenate([node_points, cotangent], axis=0).reshape(6, units, TILE)
    ctl = jnp.concatenate([ctl_points, ctl_weights], axis=0).reshape(6, part)
    for step, (node_bit, ctl_bit) in enumerate(zip(NODE_BITS, CTL_BITS)):
        nod_new = swap(nod, "ctl", node_bit)
        ctl_new = swap(ctl, "vol", ctl_bit)
        if step == 1:
            nod_new, where, mask = lax.optimization_barrier((nod_new, where, mask))
        if step == 2:
            lists, counts = pl.pallas_call(
                functools.partial(list_kernel, units=units, stride=stride),
                out_shape=(
                    jax.ShapeDtypeStruct((2 * len(CALLS) * stride,), jnp.int32),
                    jax.ShapeDtypeStruct((2 * len(CALLS),), jnp.int32),
                ),
                in_specs=[smem, smem],
                out_specs=(smem, smem),
                name="kept_tiles",
            )(where, mask)
            nod_new, lists, counts = lax.optimization_barrier((nod_new, lists, counts))
        nod = jnp.concatenate([nod, nod_new], axis=1)
        ctl = jnp.concatenate([ctl, ctl_new], axis=1)
    nod = jnp.pad(nod, ((0, 0), (0, 8), (0, 0)))
    ctl = jnp.broadcast_to(ctl[:, :, None], (6, width, TILE))

    def pairs(call, csum):
        rows = CALLS[call][1] * units
        work = rows * TILE * width
        return pl.pallas_call(
            functools.partial(pair_kernel, call=call, stride=stride, part=part),
            out_shape=(jax.ShapeDtypeStruct((3, rows, TILE), f32), jax.ShapeDtypeStruct((6, width), f32)),
            in_specs=[smem, smem, vmem, vmem, vmem],
            out_specs=(vmem, vmem),
            scratch_shapes=[pltpu.VMEM((3, rows + 8, TILE), f32), pltpu.VMEM((6, width, TILE), f32)],
            compiler_params=pltpu.CompilerParams(vmem_limit_bytes=32 << 20),
            cost_estimate=pl.CostEstimate(flops=5000 * work, bytes_accessed=16 * work, transcendentals=work),
            name="pairs",
        )(counts, lists, nod, ctl, csum)

    mine, csum = pairs(0, jnp.zeros((6, width), f32))
    got = []
    for step in range(1, len(CALLS)):
        got = [g[:, g.shape[1] // 2 :] for g in got], [g[:, : g.shape[1] // 2] for g in got]
        sent = swap(sum(got[0], mine), "ctl", SUM_BITS[step - 1])
        mine, csum = pairs(step, csum)
        csum, sent = lax.optimization_barrier((csum, sent))
        got = got[1] + [sent]
    keep = sum(got, mine)
    ckeep = csum
    sent = []
    for step, bit in enumerate(CTL_BITS[::-1]):
        span = ckeep.shape[1] // 2
        csend = swap(ckeep[:, span:], "vol", bit)
        if sent:
            if step < len(CTL_BITS) - 1:
                csend, *sent = lax.optimization_barrier((csend, *sent))
            keep = sent[0] + sent[1]
        sent = []
        if len(CALLS) - 1 + step < len(SUM_BITS):
            size = keep.shape[1] // 2
            sent = [keep[:, :size], swap(keep[:, size:], "ctl", SUM_BITS[len(CALLS) - 1 + step])]
        if step < len(CTL_BITS) - 1:
            ckeep = ckeep[:, :span] + csend
    if sent:
        keep = sent[0] + sent[1]
    node_grad = keep.reshape(3, 1, own) * (-20.0 / math.sqrt(total_ctl))
    ckeep = ckeep[:, :span] + csend
    weight_grad = ckeep[:3].reshape(3, 1, part) * (4.0 / math.sqrt(total_nodes))
    control_grad = ckeep[3:].reshape(3, 1, part) * (20.0 / math.sqrt(total_nodes))
    return (node_grad, weight_grad, control_grad)


def solution(mesh):
    nodes = P(None, "vol", "ctl")
    ctl = P(None, "ctl", "vol")
    return jax.shard_map(
        local,
        mesh=mesh,
        in_specs=(nodes, nodes, ctl, ctl, P("vol", None, "ctl", None)),
        out_specs=(nodes, ctl, ctl),
        check_vma=False,
    )
```

```python
import functools
import math

import jax
import jax.numpy as jnp
from jax import lax
from jax.experimental import pallas as pl
from jax.experimental.pallas import tpu as pltpu
from jax.sharding import PartitionSpec as P

TILE = 128
GROUP = 4
SHIFT = 1024
NODE_BITS = (12, 2, 4, 1)
CTL_BITS = (12, 4, 2, 1)
SUM_BITS = (12, 2, 4, 1)
CALLS = ((8, 8), (0, 8))
f32 = jnp.float32


def xor_of(bits, index):
    return functools.reduce(lambda a, b: a ^ b, [bit for k, bit in enumerate(bits) if index >> k & 1], 0)


def offset(slot):
    return xor_of(SUM_BITS[::-1], slot)


def place(slot):
    return [xor_of(NODE_BITS, p) for p in range(1 << len(NODE_BITS))].index(offset(slot))


def swap(value, axis, bit):
    return lax.ppermute(value, axis, [(i, i ^ bit) for i in range(lax.axis_size(axis))])


def list_kernel(mask_ref, list_ref, *, units, stride, tall):
    lists = [(call, half) for call in range(len(CALLS)) for half in range(2)]
    found = [jnp.int32(j * stride) for j in range(len(lists))]
    mine = lax.axis_index("ctl")
    columns = [half ^ (lax.axis_index("vol") // tall) for half in range(2)]
    for i in range(max(blocks for _, blocks in CALLS)):
        live = [j for j, (call, _) in enumerate(lists) if i < CALLS[call][1]]
        rows = {}
        for j in live:
            call, half = lists[j]
            rows[j] = (mine ^ offset(CALLS[call][0] + i)) * (2 * units) + columns[half]
        for k in range(units):
            for j in live:
                call, half = lists[j]
                list_ref[found[j]] = (place(CALLS[call][0] + i) * units + k) * SHIFT + i * units + k
                found[j] = found[j] + mask_ref[rows[j] + 2 * k]
    for j in range(len(lists)):
        list_ref[len(lists) * stride + j] = found[j] - j * stride


def pair_kernel(list_ref, nod_ref, ctl_ref, before_ref, part_ref, csum_ref, node_ref, acc_ref, *, call, stride, part):
    node_ref[...] = jnp.zeros_like(node_ref)
    acc_ref[...] = jnp.zeros_like(acc_ref)
    for half in range(2):
        row = 2 * call + half
        starts = [s for s in range(0, acc_ref.shape[1], 8) if s // part % 2 == half]

        def body(first, size, row=row, starts=starts):
            items = [list_ref[row * stride + first + b] for b in range(size)]
            ts = [item >> 10 for item in items]
            outs = [item & (SHIFT - 1) for item in items]
            xg = [[jnp.broadcast_to(nod_ref[k, pl.ds(t, 1), :], (8, TILE)) for k in range(6)] for t in ts]
            node_sum = [[None] * 3 for _ in range(size)]
            for c, start in enumerate(starts):
                rows = pl.ds(start, 8)
                yw = [ctl_ref[k, rows, :] for k in range(6)]
                ctl_sum = [None] * 6
                for b in range(size):
                    x = xg[b][:3]
                    g = xg[b][3:]
                    diff = [x[k] - yw[k] for k in range(3)]
                    square = diff[0] * diff[0] + diff[1] * diff[1] + diff[2] * diff[2]
                    dist = pl.reciprocal(lax.rsqrt(square), approx=True)
                    near = jnp.maximum(1.0 - dist, 0.0)
                    near2 = near * near
                    phi = near2 * near2 * (dist + 0.25)
                    align = g[0] * yw[3] + g[1] * yw[4] + g[2] * yw[5]
                    force = near2 * near * align
                    for k in range(3):
                        pulled = force * diff[k]
                        pushed = phi * g[k]
                        node_sum[b][k] = pulled if c == 0 else node_sum[b][k] + pulled
                        ctl_sum[3 + k] = pulled if b == 0 else ctl_sum[3 + k] + pulled
                        ctl_sum[k] = pushed if b == 0 else ctl_sum[k] + pushed
                for k in range(6):
                    acc_ref[k, rows, :] += ctl_sum[k]
            for b in range(size):
                for k in range(3):
                    node_ref[k, pl.ds(outs[b], 1), :] += jnp.sum(node_sum[b][k], axis=0, keepdims=True)

        def group(i, _, body=body):
            body(i * GROUP, GROUP)
            return 0

        def single(i, _, body=body):
            body(i, 1)
            return 0

        count = list_ref[2 * len(CALLS) * stride + row]
        lax.fori_loop(0, count // GROUP, group, 0)
        lax.fori_loop(count // GROUP * GROUP, count, single, 0)
    part_ref[...] = node_ref[:, : part_ref.shape[1], :]
    for k in range(6):
        for s in range(0, acc_ref.shape[1], TILE):
            total = jnp.sum(acc_ref[k, pl.ds(s, TILE), :].T, axis=0, keepdims=True)
            csum_ref[k, :, pl.ds(s, TILE)] = before_ref[k, :, pl.ds(s, TILE)] + total


def local(node_points, cotangent, ctl_points, ctl_weights, tile_mask):
    n_vol = lax.axis_size("vol")
    n_ctl = lax.axis_size("ctl")
    own = node_points.shape[2]
    units = own // TILE
    tiles = units * n_ctl
    part = ctl_points.shape[2]
    width = part * n_vol
    total_nodes = own * n_ctl * n_vol
    total_ctl = width * n_ctl
    vmem = pl.BlockSpec(memory_space=pltpu.VMEM)
    smem = pl.BlockSpec(memory_space=pltpu.SMEM)
    stride = max(blocks for _, blocks in CALLS) * units + 8
    mask = tile_mask.reshape(2 * tiles)

    nod = jnp.concatenate([node_points, cotangent], axis=0).reshape(6, units, TILE)
    ctl = jnp.concatenate([ctl_points, ctl_weights], axis=0)
    for step, (node_bit, ctl_bit) in enumerate(zip(NODE_BITS, CTL_BITS)):
        nod_new = swap(nod, "ctl", node_bit)
        ctl_new = swap(ctl, "vol", ctl_bit)
        if step == 1:
            nod_new, mask = lax.optimization_barrier((nod_new, mask))
        if step == 2:
            lists = pl.pallas_call(
                functools.partial(list_kernel, units=units, stride=stride, tall=TILE // part),
                out_shape=jax.ShapeDtypeStruct((2 * len(CALLS) * (stride + 1),), jnp.int32),
                in_specs=[smem],
                out_specs=smem,
                name="kept_tiles",
            )(mask)
            nod_new, lists = lax.optimization_barrier((nod_new, lists))
        nod = jnp.concatenate([nod, nod_new], axis=1)
        ctl = jnp.concatenate([ctl, ctl_new], axis=2)
    nod = jnp.pad(nod, ((0, 0), (0, 8), (0, 0)))
    ctl = jnp.broadcast_to(ctl.reshape(6, width, 1), (6, width, TILE))

    def pairs(call, csum):
        rows = CALLS[call][1] * units
        work = rows * TILE * width
        return pl.pallas_call(
            functools.partial(pair_kernel, call=call, stride=stride, part=part),
            out_shape=(jax.ShapeDtypeStruct((3, rows, TILE), f32), jax.ShapeDtypeStruct((6, 1, width), f32)),
            in_specs=[smem, vmem, vmem, vmem],
            out_specs=(vmem, vmem),
            scratch_shapes=[pltpu.VMEM((3, rows + 8, TILE), f32), pltpu.VMEM((6, width, TILE), f32)],
            compiler_params=pltpu.CompilerParams(vmem_limit_bytes=32 << 20),
            cost_estimate=pl.CostEstimate(flops=5000 * work, bytes_accessed=16 * work, transcendentals=work),
            name="pairs",
        )(lists, nod, ctl, csum)

    mine, csum = pairs(0, jnp.zeros((6, 1, width), f32))
    got = []
    for step in range(1, len(CALLS)):
        got = [g[:, g.shape[1] // 2 :] for g in got], [g[:, : g.shape[1] // 2] for g in got]
        sent = swap(sum(got[0], mine), "ctl", SUM_BITS[step - 1])
        mine, csum = pairs(step, csum)
        csum, sent = lax.optimization_barrier((csum, sent))
        got = got[1] + [sent]
    keep = sum(got, mine)
    ckeep = csum
    sent = []
    for step, bit in enumerate(CTL_BITS[::-1]):
        span = ckeep.shape[2] // 2
        csend = swap(ckeep[:, :, span:], "vol", bit)
        if sent:
            if step < len(CTL_BITS) - 1:
                csend, *sent = lax.optimization_barrier((csend, *sent))
            keep = sent[0] + sent[1]
        sent = []
        if len(CALLS) - 1 + step < len(SUM_BITS):
            size = keep.shape[1] // 2
            sent = [keep[:, :size], swap(keep[:, size:], "ctl", SUM_BITS[len(CALLS) - 1 + step])]
        if step < len(CTL_BITS) - 1:
            ckeep = ckeep[:, :, :span] + csend
    if sent:
        keep = sent[0] + sent[1]
    node_grad = keep.reshape(3, 1, own) * (-20.0 / math.sqrt(total_ctl))
    ckeep = ckeep[:, :, :span] + csend
    weight_grad = ckeep[:3] * (4.0 / math.sqrt(total_nodes))
    control_grad = ckeep[3:] * (20.0 / math.sqrt(total_nodes))
    return (node_grad, weight_grad, control_grad)


def solution(mesh):
    nodes = P(None, "vol", "ctl")
    ctl = P(None, "ctl", "vol")
    return jax.shard_map(
        local,
        mesh=mesh,
        in_specs=(nodes, nodes, ctl, ctl, P("vol", None, "ctl", None)),
        out_specs=(nodes, ctl, ctl),
        check_vma=False,
    )
```

```python
import functools
import math

import jax
import jax.numpy as jnp
from jax import lax
from jax.experimental import pallas as pl
from jax.experimental.pallas import tpu as pltpu
from jax.sharding import PartitionSpec as P

TILE = 128
GROUP = 4
SHIFT = 1024
NODE_BITS = (12, 2, 4, 1)
CTL_BITS = (12, 4, 2, 1)
SUM_BITS = (12, 2, 4, 1)
CALLS = ((8, 8), (0, 8))
f32 = jnp.float32


def xor_of(bits, index):
    return functools.reduce(lambda a, b: a ^ b, [bit for k, bit in enumerate(bits) if index >> k & 1], 0)


def offset(slot):
    return xor_of(SUM_BITS[::-1], slot)


def place(slot):
    return [xor_of(NODE_BITS, p) for p in range(1 << len(NODE_BITS))].index(offset(slot))


def swap(value, axis, bit):
    return lax.ppermute(value, axis, [(i, i ^ bit) for i in range(lax.axis_size(axis))])


def list_kernel(mask_ref, list_ref, *, units, stride, tall):
    lists = [(call, half) for call in range(len(CALLS)) for half in range(2)]
    found = [jnp.int32(j * stride) for j in range(len(lists))]
    mine = lax.axis_index("ctl")
    columns = [half ^ (lax.axis_index("vol") // tall) for half in range(2)]
    for i in range(max(blocks for _, blocks in CALLS)):
        live = [j for j, (call, _) in enumerate(lists) if i < CALLS[call][1]]
        rows = {}
        for j in live:
            call, half = lists[j]
            row = (mine ^ offset(CALLS[call][0] + i)) * units
            rows[j] = (row // TILE, columns[half], row % TILE)
        for k in range(units):
            for j in live:
                call, half = lists[j]
                list_ref[found[j]] = (place(CALLS[call][0] + i) * units + k) * SHIFT + i * units + k
                found[j] = found[j] + mask_ref[rows[j][0], rows[j][1], rows[j][2] + k]
    for j in range(len(lists)):
        list_ref[len(lists) * stride + j] = found[j] - j * stride


def pair_kernel(list_ref, nod_ref, ctl_ref, before_ref, part_ref, csum_ref, node_ref, acc_ref, *, call, stride, part):
    node_ref[...] = jnp.zeros_like(node_ref)
    acc_ref[...] = jnp.zeros_like(acc_ref)
    for half in range(2):
        row = 2 * call + half
        starts = [s for s in range(0, acc_ref.shape[1], 8) if s // part % 2 == half]

        def body(first, size, row=row, starts=starts):
            items = [list_ref[row * stride + first + b] for b in range(size)]
            ts = [item >> 10 for item in items]
            outs = [item & (SHIFT - 1) for item in items]
            xg = [[jnp.broadcast_to(nod_ref[k, pl.ds(t, 1), :], (8, TILE)) for k in range(6)] for t in ts]
            node_sum = [[None] * 3 for _ in range(size)]
            for c, start in enumerate(starts):
                rows = pl.ds(start, 8)
                yw = [ctl_ref[k, rows, :] for k in range(6)]
                ctl_sum = [None] * 6
                for b in range(size):
                    x = xg[b][:3]
                    g = xg[b][3:]
                    diff = [x[k] - yw[k] for k in range(3)]
                    square = diff[0] * diff[0] + diff[1] * diff[1] + diff[2] * diff[2]
                    dist = pl.reciprocal(lax.rsqrt(square), approx=True)
                    near = jnp.maximum(1.0 - dist, 0.0)
                    near2 = near * near
                    phi = near2 * near2 * (dist + 0.25)
                    align = g[0] * yw[3] + g[1] * yw[4] + g[2] * yw[5]
                    force = near2 * near * align
                    for k in range(3):
                        pulled = force * diff[k]
                        pushed = phi * g[k]
                        node_sum[b][k] = pulled if c == 0 else node_sum[b][k] + pulled
                        ctl_sum[3 + k] = pulled if b == 0 else ctl_sum[3 + k] + pulled
                        ctl_sum[k] = pushed if b == 0 else ctl_sum[k] + pushed
                for k in range(6):
                    acc_ref[k, rows, :] += ctl_sum[k]
            for b in range(size):
                for k in range(3):
                    node_ref[k, pl.ds(outs[b], 1), :] += jnp.sum(node_sum[b][k], axis=0, keepdims=True)

        def group(i, _, body=body):
            body(i * GROUP, GROUP)
            return 0

        def single(i, _, body=body):
            body(i, 1)
            return 0

        count = list_ref[2 * len(CALLS) * stride + row]
        lax.fori_loop(0, count // GROUP, group, 0)
        lax.fori_loop(count // GROUP * GROUP, count, single, 0)
    part_ref[...] = node_ref[:, : part_ref.shape[1], :]
    for k in range(6):
        for s in range(0, acc_ref.shape[1], TILE):
            total = jnp.sum(acc_ref[k, pl.ds(s, TILE), :].T, axis=0, keepdims=True)
            csum_ref[k, :, pl.ds(s, TILE)] = before_ref[k, :, pl.ds(s, TILE)] + total


def local(node_points, cotangent, ctl_points, ctl_weights, tile_mask):
    n_vol = lax.axis_size("vol")
    n_ctl = lax.axis_size("ctl")
    own = node_points.shape[2]
    units = own // TILE
    tiles = units * n_ctl
    part = ctl_points.shape[2]
    width = part * n_vol
    total_nodes = own * n_ctl * n_vol
    total_ctl = width * n_ctl
    vmem = pl.BlockSpec(memory_space=pltpu.VMEM)
    smem = pl.BlockSpec(memory_space=pltpu.SMEM)
    stride = max(blocks for _, blocks in CALLS) * units + 8
    mask = tile_mask.reshape(tiles, 2).T.reshape(2, tiles // TILE, TILE).transpose(1, 0, 2)

    nod = jnp.concatenate([node_points, cotangent], axis=0).reshape(6, units, TILE)
    ctl = jnp.concatenate([ctl_points, ctl_weights], axis=0)
    for step, (node_bit, ctl_bit) in enumerate(zip(NODE_BITS, CTL_BITS)):
        nod_new = swap(nod, "ctl", node_bit)
        ctl_new = swap(ctl, "vol", ctl_bit)
        if step == 1:
            nod_new, mask = lax.optimization_barrier((nod_new, mask))
        if step == 2:
            lists = pl.pallas_call(
                functools.partial(list_kernel, units=units, stride=stride, tall=TILE // part),
                out_shape=jax.ShapeDtypeStruct((2 * len(CALLS) * (stride + 1),), jnp.int32),
                in_specs=[smem],
                out_specs=smem,
                name="kept_tiles",
            )(mask)
            nod_new, lists = lax.optimization_barrier((nod_new, lists))
        nod = jnp.concatenate([nod, nod_new], axis=1)
        ctl = jnp.concatenate([ctl, ctl_new], axis=2)
    nod = jnp.pad(nod, ((0, 0), (0, 8), (0, 0)))
    ctl = jnp.broadcast_to(ctl.reshape(6, width, 1), (6, width, TILE))

    def pairs(call, csum):
        rows = CALLS[call][1] * units
        work = rows * TILE * width
        return pl.pallas_call(
            functools.partial(pair_kernel, call=call, stride=stride, part=part),
            out_shape=(jax.ShapeDtypeStruct((3, rows, TILE), f32), jax.ShapeDtypeStruct((6, 1, width), f32)),
            in_specs=[smem, vmem, vmem, vmem],
            out_specs=(vmem, vmem),
            scratch_shapes=[pltpu.VMEM((3, rows + 8, TILE), f32), pltpu.VMEM((6, width, TILE), f32)],
            compiler_params=pltpu.CompilerParams(vmem_limit_bytes=32 << 20),
            cost_estimate=pl.CostEstimate(flops=5000 * work, bytes_accessed=16 * work, transcendentals=work),
            name="pairs",
        )(lists, nod, ctl, csum)

    mine, csum = pairs(0, jnp.zeros((6, 1, width), f32))
    got = []
    for step in range(1, len(CALLS)):
        got = [g[:, g.shape[1] // 2 :] for g in got], [g[:, : g.shape[1] // 2] for g in got]
        sent = swap(sum(got[0], mine), "ctl", SUM_BITS[step - 1])
        mine, csum = pairs(step, csum)
        csum, sent = lax.optimization_barrier((csum, sent))
        got = got[1] + [sent]
    keep = sum(got, mine)
    ckeep = csum
    sent = []
    for step, bit in enumerate(CTL_BITS[::-1]):
        span = ckeep.shape[2] // 2
        csend = swap(ckeep[:, :, span:], "vol", bit)
        if sent:
            if step < len(CTL_BITS) - 1:
                csend, *sent = lax.optimization_barrier((csend, *sent))
            keep = sent[0] + sent[1]
        sent = []
        if len(CALLS) - 1 + step < len(SUM_BITS):
            size = keep.shape[1] // 2
            sent = [keep[:, :size], swap(keep[:, size:], "ctl", SUM_BITS[len(CALLS) - 1 + step])]
        if step < len(CTL_BITS) - 1:
            ckeep = ckeep[:, :, :span] + csend
    if sent:
        keep = sent[0] + sent[1]
    node_grad = keep.reshape(3, 1, own) * (-20.0 / math.sqrt(total_ctl))
    ckeep = ckeep[:, :, :span] + csend
    weight_grad = ckeep[:3] * (4.0 / math.sqrt(total_nodes))
    control_grad = ckeep[3:] * (20.0 / math.sqrt(total_nodes))
    return (node_grad, weight_grad, control_grad)


def solution(mesh):
    nodes = P(None, "vol", "ctl")
    ctl = P(None, "ctl", "vol")
    return jax.shard_map(
        local,
        mesh=mesh,
        in_specs=(nodes, nodes, ctl, ctl, P("vol", None, "ctl", None)),
        out_specs=(nodes, ctl, ctl),
        check_vma=False,
    )
```
